32 devices in a mesh: dp: 4 (over z), tensor: 4 (over y, x), adapter: 2 (over core).
Axes of the slice: x: 2, y: 2, z: 4, core: 2. Of those that a mesh axis runs over, the one named last changes fastest.
Arguments:
- tokens: bfloat16 [4096, 8192], P('dp', 'tensor'), may hold values from -6 to 6
- frozen_weight: bfloat16 [8192, 2048], P(None, 'tensor'), may hold values from -0.0625 to 0.0625
- adapter_down_weight: bfloat16 [64, 64, 8192], P('adapter', None, 'tensor'), may hold values from -0.0625 to 0.0625
- adapter_up_weight: bfloat16 [64, 64, 2048], P('adapter', None, 'tensor'), may hold values from -0.75 to 0.75
- output_cotangent: bfloat16 [4096, 2048], P('dp', 'tensor'), may hold values from -6 to 6
- principle_per_block: int32 [32], P('dp'), may hold values from 0 to 63
- live_block_rows: int32 [32], P('dp'), may hold values from 16 to 128, as said below
Outputs:
- adapted_output: bfloat16 [4096, 2048], P('dp', 'tensor')
- hidden_input_gradient: bfloat16 [4096, 8192], P('dp', 'tensor')
- down_map_gradient: float32 [64, 64, 8192], P('adapter', 'dp', 'tensor')
- up_map_gradient: float32 [64, 64, 2048], P('adapter', 'dp', 'tensor')
The draws below stay inside these ranges and needn't reach their ends.
Inputs may be any that keep to these rules, and one draw needn't show every extreme that they name: `live_block_rows`: between 16 and 128; the first block of each index of dp is full.
All inputs are finite; a program needn't handle non-finite values.
Results may differ from the reference program's by a relative error of at most 0.014.
Values may be sent and summed in bfloat16 or wider, within the bound.
A program may use at most 192 MiB of HBM per device.

```python
import math
import jax
import jax.numpy as jnp
import numpy as np
from jax import lax

MODEL_WIDTH = 8192
KV_OUTPUT_WIDTH = 2048
ADAPTER_RANK = 64
PRINCIPLE_COUNT = 64
BLOCK = 128
TOK_DEV = 1024
ROWS = 4096
BLOCKS = 32
N_TENSOR = 4


def draw_live_block_rows(key, part):
    key = jax.random.fold_in(key, 7)
    counts = jax.random.randint(key, (BLOCKS,), BLOCK // 8, BLOCK + 1)
    first = jnp.arange(BLOCKS) % (TOK_DEV // BLOCK) == 0
    return jnp.where(first, BLOCK, counts).astype(jnp.int32)


def set_ends(entries, own_key, low, high):
    spot = [jax.random.randint(jax.random.fold_in(own_key, axis), (), 0, length) for axis, length in enumerate(entries.shape)]
    main_axis = entries.shape.index(max(entries.shape))
    next_to = spot[:main_axis] + [(spot[main_axis] + 1) % entries.shape[main_axis]] + spot[main_axis + 1:]
    return entries.at[tuple(spot)].set(low).at[tuple(next_to)].set(high)


def block_levels(rng, shape, pieces, least, high):
    level, own = 1.0, jax.random.fold_in(rng, 6)
    for axis_at, blocks in pieces:
        heights = jnp.exp(jax.random.uniform(jax.random.fold_in(own, axis_at), (blocks,), jnp.float32, least / len(pieces), high / len(pieces)))
        level = level * jnp.repeat(heights, shape[axis_at] // blocks).reshape([-1 if axis == axis_at else 1 for axis in range(len(shape))])
    return level


def rank_table(amount, lean):
    weights = [(1 << 20) // math.isqrt(standing ** lean) + 1 for standing in range(1, amount + 1)]
    deviation = 1 + sum(weights) // (1 << 30)
    return np.cumsum(np.array([max(1, weight // deviation) for weight in weights]))


def ranked_ids(stream_key, shape, amount, slope):
    grid = rank_table(amount, slope)
    ticket = jax.random.randint(jax.random.fold_in(stream_key, 1), shape, 0, int(grid[amount - 1]))
    rank = jnp.searchsorted(jnp.asarray(grid, jnp.int32), ticket, side="right")
    return jax.random.permutation(jax.random.fold_in(stream_key, 2), amount)[rank].astype(jnp.int32)


def normal_values(own_key, extent, scale, most, cuts=(), held_as=jnp.bfloat16):
    array = jax.random.normal(own_key, extent, jnp.float32) * scale
    if len(cuts) > 0:
        array = block_levels(own_key, extent, cuts, -0.22, 0.18) * array
    return jnp.clip(array, min=-most, max=most).astype(held_as)


def setup_inputs(seed: int = 0) -> dict:
    keys = jax.random.split(jax.random.key(seed), 8)
    tokens = normal_values(keys[0], (ROWS, MODEL_WIDTH), 1.0, 6.0, ((0, 4), (1, 4)))
    frozen_weight = normal_values(keys[1], (MODEL_WIDTH, KV_OUTPUT_WIDTH), MODEL_WIDTH ** -0.5, 0.0625, ((1, 4),))
    adapter_down_weight = normal_values(keys[2], (PRINCIPLE_COUNT, ADAPTER_RANK, MODEL_WIDTH), MODEL_WIDTH ** -0.5, 0.0625, ((0, 2), (2, 4)))
    adapter_up_weight = normal_values(keys[3], (PRINCIPLE_COUNT, ADAPTER_RANK, KV_OUTPUT_WIDTH), ADAPTER_RANK ** -0.5, 0.75, ((0, 2), (2, 4)))
    output_cotangent = normal_values(keys[4], (ROWS, KV_OUTPUT_WIDTH), 1.0, 6.0, ((0, 4), (1, 4)))
    principle_per_block = set_ends(ranked_ids(keys[5], (BLOCKS,), PRINCIPLE_COUNT, 2), jax.random.fold_in(keys[5], 3), 0, PRINCIPLE_COUNT - 1).astype(jnp.int32)
    live_block_rows = draw_live_block_rows(jax.random.fold_in(keys[7], 71), 0)
    return {"tokens": tokens, "frozen_weight": frozen_weight, "adapter_down_weight": adapter_down_weight, "adapter_up_weight": adapter_up_weight, "output_cotangent": output_cotangent, "principle_per_block": principle_per_block, "live_block_rows": live_block_rows}


ADAPTER_SCALE = 2.0


def reference(tokens, frozen_weight, adapter_down_weight, adapter_up_weight, output_cotangent, principle_per_block, live_block_rows):
    live_row_number = tokens.shape[0]
    blocks = live_row_number // BLOCK
    within = jnp.arange(BLOCK, dtype=jnp.int32)
    valid_row_mask = (within[None, :] < live_block_rows[:, None]).astype(jnp.float32)[:, :, None]
    selected_down_weight = jnp.take(adapter_down_weight, principle_per_block, axis=0).astype(jnp.float32)
    selected_up_weight = jnp.take(adapter_up_weight, principle_per_block, axis=0).astype(jnp.float32)
    padded_token_blocks = tokens.reshape(blocks, BLOCK, MODEL_WIDTH).astype(jnp.float32)
    gradient_token_blocks = output_cotangent.reshape(blocks, BLOCK, KV_OUTPUT_WIDTH).astype(jnp.float32)
    rank_projected_hidden = jnp.einsum('avc,amc->avm', padded_token_blocks, selected_down_weight) * valid_row_mask
    backrank = jnp.einsum('brc,bkc->brk', gradient_token_blocks, selected_up_weight) * valid_row_mask
    block_rank_state = rank_projected_hidden.astype(jnp.bfloat16).astype(jnp.float32)
    backward_block_rows = backrank.astype(jnp.bfloat16).astype(jnp.float32)
    adapter_output_delta = ADAPTER_SCALE * jnp.einsum('xyl,xlp->xyp', block_rank_state, selected_up_weight)
    frozen_output = jnp.dot(tokens, frozen_weight, preferred_element_type=jnp.float32)
    adapted_output = (frozen_output + adapter_output_delta.reshape(live_row_number, KV_OUTPUT_WIDTH)).astype(jnp.bfloat16)
    col_width = KV_OUTPUT_WIDTH // N_TENSOR
    frozen_input_grad = jnp.zeros((live_row_number, MODEL_WIDTH), jnp.float32)
    for group in range(N_TENSOR):
        grad_cols = lax.dynamic_slice_in_dim(output_cotangent, group * col_width, col_width, 1)
        weight_cols = lax.dynamic_slice_in_dim(frozen_weight, group * col_width, col_width, 1)
        group_back = lax.dot_general(grad_cols, weight_cols, (((1,), (1,)), ((), ())), preferred_element_type=jnp.float32)
        rounded = lax.optimization_barrier(group_back.astype(jnp.bfloat16))
        frozen_input_grad = frozen_input_grad + rounded.astype(jnp.float32)
    adapter_input_gradient = ADAPTER_SCALE * jnp.einsum('vis,vsy->viy', backward_block_rows, selected_down_weight).reshape(live_row_number, MODEL_WIDTH)
    hidden_input_gradient = (frozen_input_grad + adapter_input_gradient).astype(jnp.bfloat16)
    down_block_weight = ADAPTER_SCALE * jnp.einsum('szj,szy->sjy', backward_block_rows, padded_token_blocks)
    up_block_weight = ADAPTER_SCALE * jnp.einsum('vwf,vwh->vfh', block_rank_state, gradient_token_blocks)
    down_map_gradient = jnp.zeros((PRINCIPLE_COUNT, ADAPTER_RANK, MODEL_WIDTH), jnp.float32).at[principle_per_block].add(down_block_weight)
    up_map_gradient = jnp.zeros((PRINCIPLE_COUNT, ADAPTER_RANK, KV_OUTPUT_WIDTH), jnp.float32).at[principle_per_block].add(up_block_weight)
    return adapted_output, hidden_input_gradient, down_map_gradient, up_map_gradient
```

```python
import functools

import jax
import jax.numpy as jnp
from jax import lax
from jax.experimental import pallas as pl
from jax.experimental.pallas import tpu as pltpu
from jax.sharding import PartitionSpec as P

BLOCK = 128
ADAPTER_SCALE = 2.0
MESH = pl.DeviceIdType.MESH


def flip(index, distance, count):
    out, bit = 0, 1
    while bit < count:
        out = out + ((index // bit + distance // bit) % 2) * bit
        bit *= 2
    return out


def tile_of(size, most):
    return most if size % most == 0 else size


def kernel(
    num_tensor,
    num_dp,
    tok_ref,
    w_ref,
    down_ref,
    up_ref,
    cot_ref,
    pick_ref,
    own_ref,
    live_ref,
    ids_ref,
    out_ref,
    hid_ref,
    gd_ref,
    gu_ref,
    gid_ref,
    tok_v,
    wf,
    cotf,
    down_v,
    up_v,
    a_snd,
    a_rcv,
    a_own,
    b_snd,
    b_rcv,
    b_own,
    rk_snd,
    rk_rcv,
    rank_v,
    gd_snd,
    gu_snd,
    acc,
    o_zero,
    o_snd,
    o_rcv,
    o_fin,
    h_fin,
    loc_sem,
    cot_s,
    cot_r,
    w_s,
    w_r,
    wr_s,
    wr_r,
    ab_s,
    ab_r,
    rk_s,
    rk_r,
    g_s,
    g_r,
    gr_s,
    gr_r,
    o_s,
    o_r,
    fin_s,
    fin_r,
):
    z = lax.axis_index("dp")
    t = lax.axis_index("tensor")
    a = lax.axis_index("adapter")
    pa = 1 - a
    rows, d = tok_v.shape
    c = cotf.shape[2]
    half = d // 2
    nb = rows // BLOCK
    rank = down_v.shape[1]
    rk = rank // num_dp
    partner = (z, t, pa)
    my_rows = pl.ds(pl.multiple_of(a * rows, rows), rows)
    my_half = pl.ds(pl.multiple_of(a * half, half), half)

    def local(src, dst, sem):
        copy = pltpu.make_async_copy(src, dst, loc_sem.at[sem])
        copy.start()
        return copy

    def remote(src, dst, ss, rs, dev):
        copy = pltpu.make_async_remote_copy(
            src_ref=src, dst_ref=dst, send_sem=ss, recv_sem=rs, device_id=dev, device_id_type=MESH
        )
        copy.start()
        return copy

    cp_cot = local(cot_ref.at[my_rows, :], cotf.at[0], 0)
    cp_down = local(down_ref, down_v, 1)
    cp_up = local(up_ref, up_v, 2)
    cp_tok = local(tok_ref.at[my_rows, :], tok_v, 3)
    cp_w = local(w_ref.at[pl.ds(pl.multiple_of(t * d, d), d), :], wf.at[0], 4)

    tensor_peer = [None] + [(z, flip(t, k, num_tensor), a) for k in range(1, num_tensor)]
    dp_peer = [None] + [(lax.rem(z + j, num_dp), t, a) for j in range(1, num_dp)]
    barrier = pltpu.get_barrier_semaphore()
    for peer in tensor_peer[1:] + dp_peer[1:] + [partner]:
        pl.semaphore_signal(barrier, inc=1, device_id=peer, device_id_type=MESH)
    pl.semaphore_wait(barrier, num_tensor + num_dp - 1)

    cot_c, w_c = [None], [None]
    for k in range(1, num_tensor):
        cot_c.append(
            remote(cot_ref.at[my_rows, :], cotf.at[k], cot_s.at[k], cot_r.at[k], tensor_peer[k])
        )
    for k in range(1, num_tensor):
        start = pl.multiple_of(tensor_peer[k][1] * d + a * half, half)
        w_c.append(
            remote(
                w_ref.at[pl.ds(start, half), :],
                wf.at[k, my_half, :],
                w_s.at[k],
                w_r.at[k],
                tensor_peer[k],
            )
        )

    cp_down.wait()
    cp_up.wait()
    for i in range(nb):
        b = pa * nb + i
        a_snd[i] = (down_v[pick_ref[b]].astype(jnp.float32) * own_ref[b]).astype(jnp.bfloat16)
        b_snd[i] = (up_v[pick_ref[b]].astype(jnp.float32) * own_ref[b]).astype(jnp.bfloat16)
    a_c = remote(a_snd, a_rcv, ab_s.at[0], ab_r.at[0], partner)
    b_c = remote(b_snd, b_rcv, ab_s.at[1], ab_r.at[1], partner)
    for i in range(nb):
        b = a * nb + i
        a_own[i] = (down_v[pick_ref[b]].astype(jnp.float32) * own_ref[b]).astype(jnp.bfloat16)
        b_own[i] = (up_v[pick_ref[b]].astype(jnp.float32) * own_ref[b]).astype(jnp.bfloat16)
    a_c.wait_recv()
    b_c.wait_recv()
    for i in range(nb):
        a_own[i] = a_own[i] + a_rcv[i]
        b_own[i] = b_own[i] + b_rcv[i]

    cp_tok.wait()
    cp_cot.wait()
    last = (((1,), (1,)), ((), ()))
    for i in range(nb):
        blk = slice(i * BLOCK, (i + 1) * BLOCK)
        low = lax.dot_general(tok_v[blk, :], a_own[i], last, preferred_element_type=jnp.float32)
        back = lax.dot_general(cotf[0, blk, :], b_own[i], last, preferred_element_type=jnp.float32)
        rk_snd[blk, :] = jnp.concatenate([low, back], axis=1).astype(jnp.bfloat16)
    rk_c = [None]
    for k in range(1, num_tensor):
        rk_c.append(remote(rk_snd, rk_rcv.at[k], rk_s.at[k], rk_r.at[k], tensor_peer[k]))

    row_tile = tile_of(rows, 256)
    d_tile = tile_of(d, 512)

    def forward(k, store):
        @pl.loop(0, rows // row_tile)
        def _(step):
            at = pl.ds(pl.multiple_of(step * row_tile, row_tile), row_tile)
            store(at, jnp.dot(tok_v[at, :], wf[k], preferred_element_type=jnp.float32))

    def backward(k):
        @pl.loop(0, d // d_tile)
        def _(step):
            at = pl.ds(pl.multiple_of(step * d_tile, d_tile), d_tile)
            part = lax.dot_general(cotf[k], wf[k, at, :], last, preferred_element_type=jnp.float32)
            part = part.astype(jnp.bfloat16).astype(jnp.float32)
            acc[:, at] = part if k == 0 else acc[:, at] + part

    def store_zero(at, value):
        o_zero[at, :] = value

    cp_w.wait()
    forward(0, store_zero)
    backward(0)

    for k in range(1, num_tensor):
        rk_c[k].wait_recv()
    within = lax.broadcasted_iota(jnp.int32, (BLOCK, 2 * rank), 0)
    for i in range(nb):
        blk = slice(i * BLOCK, (i + 1) * BLOCK)
        total = rk_snd[blk, :].astype(jnp.float32)
        for k in range(1, num_tensor):
            total = total + rk_rcv[k, blk, :].astype(jnp.float32)
        total = jnp.where(within < live_ref[a * nb + i], total, 0.0)
        rank_v[blk, :] = total.astype(jnp.bfloat16)
        turned = total.T.astype(jnp.bfloat16)
        gd = jnp.dot(turned[rank:], tok_v[blk, :], preferred_element_type=jnp.float32)
        gu = jnp.dot(turned[:rank], cotf[0, blk, :], preferred_element_type=jnp.float32)
        gd = ADAPTER_SCALE * gd
        gu = ADAPTER_SCALE * gu
        for j in range(num_dp):
            part = slice(i * rk, (i + 1) * rk)
            gd_snd[j, part, :] = gd[j * rk : (j + 1) * rk].astype(jnp.bfloat16)
            gu_snd[j, part, :] = gu[j * rk : (j + 1) * rk].astype(jnp.bfloat16)
    g_c = [None]
    for j in range(1, num_dp):
        to = dp_peer[j][0]
        g_c.append(
            (
                remote(gd_snd.at[to], gd_ref.at[z, a], g_s.at[0, j], g_r.at[0, j], dp_peer[j]),
                remote(gu_snd.at[to], gu_ref.at[z, a], g_s.at[1, j], g_r.at[1, j], dp_peer[j]),
                remote(ids_ref, gid_ref.at[z], g_s.at[2, j], g_r.at[2, j], dp_peer[j]),
            )
        )
    cp_gd = local(gd_snd.at[z], gd_ref.at[z, a], 5)
    cp_gu = local(gu_snd.at[z], gu_ref.at[z, a], 6)
    cp_id = local(ids_ref, gid_ref.at[z], 7)
    gr_c = [
        (
            remote(gd_snd.at[z], gd_ref.at[z, a], gr_s.at[0, 0], gr_r.at[0, 0], partner),
            remote(gu_snd.at[z], gu_ref.at[z, a], gr_s.at[1, 0], gr_r.at[1, 0], partner),
        )
    ]

    wr_c = [None] * num_tensor
    o_c = [None] * num_tensor

    def relay(k):
        w_c[k].wait_recv()
        wr_c[k] = remote(
            wf.at[k, my_half, :], wf.at[k, my_half, :], wr_s.at[k], wr_r.at[k], partner
        )

    relay(1)
    for k in range(1, num_tensor):
        if k + 1 < num_tensor and k < 2:
            relay(k + 1)
        wr_c[k].wait_recv()

        def store_send(at, value, k=k):
            o_snd[k, at, :] = value.astype(jnp.bfloat16)

        forward(k, store_send)
        o_c[k] = remote(o_snd.at[k], o_rcv.at[k], o_s.at[k], o_r.at[k], tensor_peer[k])
        if k >= 2 and k + 1 < num_tensor:
            relay(k + 1)
        cot_c[k].wait_recv()
        backward(k)

    for i in range(nb):
        blk = slice(i * BLOCK, (i + 1) * BLOCK)
        low_b = rank_v[blk, :rank]
        back_b = rank_v[blk, rank:]
        term = jnp.dot(back_b, a_own[i], preferred_element_type=jnp.float32)
        h_fin[blk, :] = (acc[blk, :] + ADAPTER_SCALE * term).astype(jnp.bfloat16)
        o_term = jnp.dot(low_b, b_own[i], preferred_element_type=jnp.float32)
        o_zero[blk, :] = o_zero[blk, :] + ADAPTER_SCALE * o_term
    h_c = remote(h_fin, hid_ref.at[my_rows, :], fin_s.at[0], fin_r.at[0], partner)
    cp_h = local(h_fin, hid_ref.at[my_rows, :], 8)

    for j in range(1, num_dp):
        for copy in g_c[j]:
            copy.wait_recv()
        source = lax.rem(z + num_dp - j, num_dp)
        mine_d, mine_u = gd_ref.at[source, a], gu_ref.at[source, a]
        gr_c.append(
            (
                remote(mine_d, mine_d, gr_s.at[0, j], gr_r.at[0, j], partner),
                remote(mine_u, mine_u, gr_s.at[1, j], gr_r.at[1, j], partner),
            )
        )

    for k in range(1, num_tensor):
        o_c[k].wait_recv()
    for i in range(nb):
        blk = slice(i * BLOCK, (i + 1) * BLOCK)
        total = o_zero[blk, :]
        for k in range(1, num_tensor):
            total = total + o_rcv[k, blk, :].astype(jnp.float32)
        o_fin[blk, :] = total.astype(jnp.bfloat16)
    of_c = remote(o_fin, out_ref.at[my_rows, :], fin_s.at[1], fin_r.at[1], partner)
    cp_o = local(o_fin, out_ref.at[my_rows, :], 9)

    for copy in (cp_gd, cp_gu, cp_id, cp_h, cp_o):
        copy.wait()
    for k in range(1, num_tensor):
        cot_c[k].wait_send()
        w_c[k].wait_send()
        rk_c[k].wait_send()
        wr_c[k].wait_send()
        o_c[k].wait_send()
    a_c.wait_send()
    b_c.wait_send()
    for j in range(1, num_dp):
        for copy in g_c[j]:
            copy.wait_send()
    for pair in gr_c:
        for copy in pair:
            copy.wait()
    h_c.wait()
    of_c.wait()


def on_device(
    num_tensor,
    num_dp,
    tokens,
    frozen_weight,
    adapter_down_weight,
    adapter_up_weight,
    output_cotangent,
    principle_per_block,
    live_block_rows,
):
    all_rows, d = tokens.shape
    c = frozen_weight.shape[1]
    principles, rank = adapter_down_weight.shape[:2]
    blocks = all_rows // BLOCK
    rows, nb, rk = all_rows // 2, blocks // 2, rank // num_dp
    core = lax.axis_index("adapter")
    local_pick = principle_per_block - core * principles
    owned = ((local_pick >= 0) & (local_pick < principles)).astype(jnp.float32)
    pick = jnp.clip(local_pick, 0, principles - 1)
    ids = jnp.broadcast_to(principle_per_block.astype(jnp.float32)[:, None], (blocks, 128))

    bf, f32 = jnp.bfloat16, jnp.float32
    hbm = pl.BlockSpec(memory_space=pl.ANY)
    smem = pl.BlockSpec(memory_space=pltpu.SMEM)
    dma = pltpu.SemaphoreType.DMA
    T, Z = num_tensor, num_dp
    out, hidden, gd, gu, gid = pl.pallas_call(
        functools.partial(kernel, T, Z),
        out_shape=(
            jax.ShapeDtypeStruct((all_rows, c), bf),
            jax.ShapeDtypeStruct((all_rows, d), bf),
            jax.ShapeDtypeStruct((Z, 2, nb * rk, d), bf),
            jax.ShapeDtypeStruct((Z, 2, nb * rk, c), bf),
            jax.ShapeDtypeStruct((Z, blocks, 128), f32),
        ),
        in_specs=[hbm] * 5 + [smem] * 3 + [hbm],
        out_specs=[hbm] * 5,
        scratch_shapes=[
            pltpu.VMEM((rows, d), bf),
            pltpu.VMEM((T, d, c), bf),
            pltpu.VMEM((T, rows, c), bf),
            pltpu.VMEM((principles, rank, d), bf),
            pltpu.VMEM((principles, rank, c), bf),
            pltpu.VMEM((nb, rank, d), bf),
            pltpu.VMEM((nb, rank, d), bf),
            pltpu.VMEM((nb, rank, d), bf),
            pltpu.VMEM((nb, rank, c), bf),
            pltpu.VMEM((nb, rank, c), bf),
            pltpu.VMEM((nb, rank, c), bf),
            pltpu.VMEM((rows, 2 * rank), bf),
            pltpu.VMEM((T, rows, 2 * rank), bf),
            pltpu.VMEM((rows, 2 * rank), bf),
            pltpu.VMEM((Z, nb * rk, d), bf),
            pltpu.VMEM((Z, nb * rk, c), bf),
            pltpu.VMEM((rows, d), f32),
            pltpu.VMEM((rows, c), f32),
            pltpu.VMEM((T, rows, c), bf),
            pltpu.VMEM((T, rows, c), bf),
            pltpu.VMEM((rows, c), bf),
            pltpu.VMEM((rows, d), bf),
            dma((10,)),
            dma((T,)),
            dma((T,)),
            dma((T,)),
            dma((T,)),
            dma((T,)),
            dma((T,)),
            dma((2,)),
            dma((2,)),
            dma((T,)),
            dma((T,)),
            dma((3, Z)),
            dma((3, Z)),
            dma((2, Z)),
            dma((2, Z)),
            dma((T,)),
            dma((T,)),
            dma((2,)),
            dma((2,)),
        ],
        compiler_params=pltpu.CompilerParams(
            collective_id=0, has_side_effects=True, vmem_limit_bytes=56 * 1024 * 1024
        ),
        cost_estimate=pl.CostEstimate(
            flops=4 * rows * d * c * T, bytes_accessed=8 * d * c * T, transcendentals=0
        ),
    )(
        tokens,
        frozen_weight,
        adapter_down_weight,
        adapter_up_weight,
        output_cotangent,
        pick,
        owned,
        live_block_rows,
        ids,
    )
    slots = core * principles + jnp.arange(principles, dtype=jnp.int32)
    chosen = (slots[:, None].astype(f32) == gid[:, :, 0].reshape(1, -1)).astype(bf)
    gd = gd.reshape(Z * blocks, rk, d)
    gu = gu.reshape(Z * blocks, rk, c)
    down_map_gradient = jnp.einsum("pb,bkd->pkd", chosen, gd, preferred_element_type=f32)
    up_map_gradient = jnp.einsum("pb,bkd->pkd", chosen, gu, preferred_element_type=f32)
    return out, hidden, down_map_gradient, up_map_gradient


def solution(mesh):
    in_specs = (
        P("dp", "tensor"),
        P(None, "tensor"),
        P("adapter", None, "tensor"),
        P("adapter", None, "tensor"),
        P("dp", "tensor"),
        P("dp"),
        P("dp"),
    )
    out_specs = (
        P("dp", "tensor"),
        P("dp", "tensor"),
        P("adapter", "dp", "tensor"),
        P("adapter", "dp", "tensor"),
    )
    return jax.shard_map(
        functools.partial(on_device, mesh.shape["tensor"], mesh.shape["dp"]),
        mesh=mesh,
        in_specs=in_specs,
        out_specs=out_specs,
        check_vma=False,
    )
```

```python
import functools

import jax
import jax.numpy as jnp
from jax import lax
from jax.experimental import pallas as pl
from jax.experimental.pallas import tpu as pltpu
from jax.sharding import PartitionSpec as P

BLOCK = 128
ADAPTER_SCALE = 2.0
MESH = pl.DeviceIdType.MESH


def flip(index, distance, count):
    out, bit = 0, 1
    while bit < count:
        out = out + ((index // bit + distance // bit) % 2) * bit
        bit *= 2
    return out


def tile_of(size, most):
    return most if size % most == 0 else size


def kernel(
    num_tensor,
    num_dp,
    tok_ref,
    w_ref,
    down_ref,
    up_ref,
    cot_ref,
    principle_ref,
    live_ref,
    out_ref,
    hid_ref,
    dmap_ref,
    umap_ref,
    tok_v,
    wf,
    cotf,
    down_v,
    up_v,
    a_snd,
    a_rcv,
    a_own,
    b_snd,
    b_rcv,
    b_own,
    rk_snd,
    rk_rcv,
    rank_v,
    gd_snd,
    gu_snd,
    ids_v,
    gdf,
    guf,
    gid,
    dmap_v,
    umap_v,
    acc,
    o_zero,
    o_snd,
    o_rcv,
    o_fin,
    h_fin,
    loc_sem,
    cot_s,
    cot_r,
    cf_s,
    cf_r,
    w_s,
    w_r,
    wz_s,
    wz_r,
    wr_s,
    wr_r,
    ab_s,
    ab_r,
    rk_s,
    rk_r,
    g_s,
    g_r,
    gr_s,
    gr_r,
    o_s,
    o_r,
    fin_s,
    fin_r,
):
    z = lax.axis_index("dp")
    t = lax.axis_index("tensor")
    a = lax.axis_index("adapter")
    pa = 1 - a
    rows, d = tok_v.shape
    c = cotf.shape[2]
    half = d // 2
    nb = rows // BLOCK
    principles, rank = down_v.shape[:2]
    rk = rank // num_dp
    partner = (z, t, pa)
    my_rows = pl.ds(pl.multiple_of(a * rows, rows), rows)
    my_half = pl.ds(pl.multiple_of(a * half, half), half)

    def local(src, dst, sem):
        copy = pltpu.make_async_copy(src, dst, loc_sem.at[sem])
        copy.start()
        return copy

    def remote(src, dst, ss, rs, dev):
        copy = pltpu.make_async_remote_copy(
            src_ref=src, dst_ref=dst, send_sem=ss, recv_sem=rs, device_id=dev, device_id_type=MESH
        )
        copy.start()
        return copy

    cp_cot = local(cot_ref.at[my_rows, :], cotf.at[0], 0)
    cp_down = local(down_ref, down_v, 1)
    cp_up = local(up_ref, up_v, 2)
    cp_tok = local(tok_ref.at[my_rows, :], tok_v, 3)
    cp_w = local(w_ref.at[pl.ds(pl.multiple_of(t * d, d), d), :], wf.at[0], 4)

    tensor_peer = [None] + [(z, flip(t, k, num_tensor), a) for k in range(1, num_tensor)]
    dp_peer = [None] + [(lax.rem(z + j, num_dp), t, a) for j in range(1, num_dp)]
    barrier = pltpu.get_barrier_semaphore()
    for peer in tensor_peer[1:] + dp_peer[1:] + [partner]:
        pl.semaphore_signal(barrier, inc=1, device_id=peer, device_id_type=MESH)
    pl.semaphore_wait(barrier, num_tensor + num_dp - 1)

    far = num_tensor - 1
    share = half // num_dp
    my_share = pl.ds(pl.multiple_of(a * half + z * share, share), share)
    w_c = [None] * num_tensor
    far_at = pl.multiple_of(tensor_peer[far][1] * d + a * half + z * share, share)
    w_c[far] = remote(
        w_ref.at[pl.ds(far_at, share), :],
        wf.at[far, my_share, :],
        w_s.at[far],
        w_r.at[far],
        tensor_peer[far],
    )
    handed = num_tensor == 4
    cot_c = [None] * num_tensor
    for k in range(1, far if handed else num_tensor):
        cot_c[k] = remote(
            cot_ref.at[my_rows, :], cotf.at[k], cot_s.at[k], cot_r.at[k], tensor_peer[k]
        )

    def chosen(table, b):
        pick = principle_ref[b] - a * principles
        own = jnp.where((pick >= 0) & (pick < principles), 1.0, 0.0).astype(jnp.float32)
        pick = jnp.minimum(jnp.maximum(pick, 0), principles - 1)
        return (table[pick].astype(jnp.float32) * own).astype(jnp.bfloat16)

    cp_down.wait()
    cp_up.wait()
    for i in range(nb):
        a_snd[i] = chosen(down_v, pa * nb + i)
        b_snd[i] = chosen(up_v, pa * nb + i)
    a_c = remote(a_snd, a_rcv, ab_s.at[0], ab_r.at[0], partner)
    b_c = remote(b_snd, b_rcv, ab_s.at[1], ab_r.at[1], partner)
    for i in range(nb):
        a_own[i] = chosen(down_v, a * nb + i)
        b_own[i] = chosen(up_v, a * nb + i)
    for b in range(2 * nb):
        ids_v[b * rk : (b + 1) * rk, :] = jnp.full(
            (rk, 128), principle_ref[b].astype(jnp.float32), jnp.float32
        )
    w_c[far].wait_recv()
    wz_c = [None]
    for j in range(1, num_dp):
        mine = wf.at[far, my_share, :]
        wz_c.append(remote(mine, mine, wz_s.at[j], wz_r.at[j], dp_peer[j]))
    a_c.wait_recv()
    b_c.wait_recv()
    for i in range(nb):
        a_own[i] = a_own[i] + a_rcv[i]
        b_own[i] = b_own[i] + b_rcv[i]

    cp_tok.wait()
    cp_cot.wait()
    last = (((1,), (1,)), ((), ()))
    for i in range(nb):
        blk = slice(i * BLOCK, (i + 1) * BLOCK)
        low = lax.dot_general(tok_v[blk, :], a_own[i], last, preferred_element_type=jnp.float32)
        back = lax.dot_general(cotf[0, blk, :], b_own[i], last, preferred_element_type=jnp.float32)
        rk_snd[blk, :] = jnp.concatenate([low, back], axis=1).astype(jnp.bfloat16)
    rk_c = [None]
    for k in range(1, num_tensor):
        rk_c.append(remote(rk_snd, rk_rcv.at[k], rk_s.at[k], rk_r.at[k], tensor_peer[k]))
    for k in range(1, far):
        start = pl.multiple_of(tensor_peer[k][1] * d + a * half, half)
        w_c[k] = remote(
            w_ref.at[pl.ds(start, half), :],
            wf.at[k, my_half, :],
            w_s.at[k],
            w_r.at[k],
            tensor_peer[k],
        )
    cf_c = []
    if handed:
        for n, k in enumerate((1, 2)):
            cot_c[k].wait_recv()
            piece = slice(n * (rows // 2), (n + 1) * (rows // 2))
            cf_c.append(
                remote(
                    cotf.at[k, piece, :],
                    cotf.at[3, piece, :],
                    cf_s.at[n],
                    cf_r.at[n],
                    tensor_peer[3 - k],
                )
            )

    row_tile = tile_of(rows, 256)
    d_tile = tile_of(d, 512)

    def forward(k, store):
        @pl.loop(0, rows // row_tile)
        def _(step):
            at = pl.ds(pl.multiple_of(step * row_tile, row_tile), row_tile)
            store(at, jnp.dot(tok_v[at, :], wf[k], preferred_element_type=jnp.float32))

    def backward(k):
        @pl.loop(0, d // d_tile)
        def _(step):
            at = pl.ds(pl.multiple_of(step * d_tile, d_tile), d_tile)
            part = lax.dot_general(cotf[k], wf[k, at, :], last, preferred_element_type=jnp.float32)
            part = part.astype(jnp.bfloat16).astype(jnp.float32)
            acc[:, at] = part if k == 0 else acc[:, at] + part

    def store_zero(at, value):
        o_zero[at, :] = value

    cp_w.wait()
    forward(0, store_zero)
    backward(0)

    for k in range(1, num_tensor):
        rk_c[k].wait_recv()
    within = lax.broadcasted_iota(jnp.int32, (BLOCK, 2 * rank), 0)
    for i in range(nb):
        blk = slice(i * BLOCK, (i + 1) * BLOCK)
        total = rk_snd[blk, :].astype(jnp.float32)
        for k in range(1, num_tensor):
            total = total + rk_rcv[k, blk, :].astype(jnp.float32)
        total = jnp.where(within < live_ref[a * nb + i], total, 0.0)
        rank_v[blk, :] = total.astype(jnp.bfloat16)
        turned = total.T.astype(jnp.bfloat16)
        gd = jnp.dot(turned[rank:], tok_v[blk, :], preferred_element_type=jnp.float32)
        gu = jnp.dot(turned[:rank], cotf[0, blk, :], preferred_element_type=jnp.float32)
        gd = ADAPTER_SCALE * gd
        gu = ADAPTER_SCALE * gu
        for j in range(num_dp):
            part = slice(i * rk, (i + 1) * rk)
            gd_snd[j, part, :] = gd[j * rk : (j + 1) * rk].astype(jnp.bfloat16)
            gu_snd[j, part, :] = gu[j * rk : (j + 1) * rk].astype(jnp.bfloat16)
    g_c = [None]
    for j in range(1, num_dp):
        to = dp_peer[j][0]
        g_c.append(
            (
                remote(gd_snd.at[to], gdf.at[z, a], g_s.at[0, j], g_r.at[0, j], dp_peer[j]),
                remote(gu_snd.at[to], guf.at[z, a], g_s.at[1, j], g_r.at[1, j], dp_peer[j]),
                remote(ids_v, gid.at[z], g_s.at[2, j], g_r.at[2, j], dp_peer[j]),
            )
        )
    cp_gd = local(gd_snd.at[z], gdf.at[z, a], 5)
    cp_gu = local(gu_snd.at[z], guf.at[z, a], 6)
    cp_id = local(ids_v, gid.at[z], 7)
    gr_c = [
        (
            remote(gd_snd.at[z], gdf.at[z, a], gr_s.at[0, 0], gr_r.at[0, 0], partner),
            remote(gu_snd.at[z], guf.at[z, a], gr_s.at[1, 0], gr_r.at[1, 0], partner),
        )
    ]

    wr_c = [None] * num_tensor
    o_c = [None] * num_tensor

    def relay(k):
        if k == far:
            for j in range(1, num_dp):
                wz_c[j].wait_recv()
        else:
            w_c[k].wait_recv()
        wr_c[k] = remote(
            wf.at[k, my_half, :], wf.at[k, my_half, :], wr_s.at[k], wr_r.at[k], partner
        )

    relay(1)
    for k in range(1, num_tensor):
        if k + 1 < num_tensor and k < 2:
            relay(k + 1)
        wr_c[k].wait_recv()

        def store_send(at, value, k=k):
            o_snd[k, at, :] = value.astype(jnp.bfloat16)

        forward(k, store_send)
        o_c[k] = remote(o_snd.at[k], o_rcv.at[k], o_s.at[k], o_r.at[k], tensor_peer[k])
        if k >= 2 and k + 1 < num_tensor:
            relay(k + 1)
        if handed and k == far:
            for copy in cf_c:
                copy.wait_recv()
        elif not handed:
            cot_c[k].wait_recv()
        backward(k)

    for j in range(1, num_dp):
        for copy in g_c[j]:
            copy.wait_recv()
        source = lax.rem(z + num_dp - j, num_dp)
        mine_d, mine_u = gdf.at[source, a], guf.at[source, a]
        gr_c.append(
            (
                remote(mine_d, mine_d, gr_s.at[0, j], gr_r.at[0, j], partner),
                remote(mine_u, mine_u, gr_s.at[1, j], gr_r.at[1, j], partner),
            )
        )

    for i in range(nb):
        blk = slice(i * BLOCK, (i + 1) * BLOCK)
        low_b = rank_v[blk, :rank]
        back_b = rank_v[blk, rank:]
        term = jnp.dot(back_b, a_own[i], preferred_element_type=jnp.float32)
        h_fin[blk, :] = (acc[blk, :] + ADAPTER_SCALE * term).astype(jnp.bfloat16)
        o_term = jnp.dot(low_b, b_own[i], preferred_element_type=jnp.float32)
        o_zero[blk, :] = o_zero[blk, :] + ADAPTER_SCALE * o_term
    h_c = remote(h_fin, hid_ref.at[my_rows, :], fin_s.at[0], fin_r.at[0], partner)
    cp_h = local(h_fin, hid_ref.at[my_rows, :], 8)

    cp_gd.wait()
    cp_gu.wait()
    cp_id.wait()
    for pair in gr_c:
        for copy in pair:
            copy.wait_recv()
    held = num_dp * 2 * nb * rk
    width = principles * rk
    grads_d = gdf[...].reshape(held, d)
    grads_u = guf[...].reshape(held, c)
    ids = gid[...].reshape(held, 128)
    lane = lax.broadcasted_iota(jnp.int32, (held, 128), 1)
    sub = lax.broadcasted_iota(jnp.int32, (held, 128), 0)
    for part in range(width // 128):
        to = slice(part * 128, (part + 1) * 128)
        column = lane + part * 128
        slot = (a * principles + column // rk).astype(jnp.float32)
        hit = (ids == slot) & (column % rk == sub % rk)
        select = jnp.where(hit, 1.0, 0.0).astype(jnp.float32).T.astype(jnp.bfloat16)
        dmap_v[to, :] = jnp.dot(select, grads_d, preferred_element_type=jnp.float32)
        umap_v[to, :] = jnp.dot(select, grads_u, preferred_element_type=jnp.float32)
    cp_dm = local(dmap_v, dmap_ref, 10)
    cp_um = local(umap_v, umap_ref, 11)

    for k in range(1, num_tensor):
        o_c[k].wait_recv()
    for i in range(nb):
        blk = slice(i * BLOCK, (i + 1) * BLOCK)
        total = o_zero[blk, :]
        for k in range(1, num_tensor):
            total = total + o_rcv[k, blk, :].astype(jnp.float32)
        o_fin[blk, :] = total.astype(jnp.bfloat16)
    of_c = remote(o_fin, out_ref.at[my_rows, :], fin_s.at[1], fin_r.at[1], partner)
    cp_o = local(o_fin, out_ref.at[my_rows, :], 9)

    for copy in (cp_h, cp_o, cp_dm, cp_um):
        copy.wait()
    for k in range(1, num_tensor):
        if cot_c[k] is not None:
            cot_c[k].wait_send()
        w_c[k].wait_send()
        rk_c[k].wait_send()
        wr_c[k].wait_send()
        o_c[k].wait_send()
    for copy in cf_c:
        copy.wait_send()
    a_c.wait_send()
    b_c.wait_send()
    for j in range(1, num_dp):
        for copy in g_c[j]:
            copy.wait_send()
        wz_c[j].wait_send()
    for pair in gr_c:
        for copy in pair:
            copy.wait_send()
    h_c.wait()
    of_c.wait()


def on_device(
    num_tensor,
    num_dp,
    tokens,
    frozen_weight,
    adapter_down_weight,
    adapter_up_weight,
    output_cotangent,
    principle_per_block,
    live_block_rows,
):
    all_rows, d = tokens.shape
    c = frozen_weight.shape[1]
    principles, rank = adapter_down_weight.shape[:2]
    blocks = all_rows // BLOCK
    rows, nb, rk = all_rows // 2, blocks // 2, rank // num_dp
    bf, f32 = jnp.bfloat16, jnp.float32
    hbm = pl.BlockSpec(memory_space=pl.ANY)
    smem = pl.BlockSpec(memory_space=pltpu.SMEM)
    dma = pltpu.SemaphoreType.DMA
    T, Z = num_tensor, num_dp
    out, hidden, dmap, umap = pl.pallas_call(
        functools.partial(kernel, T, Z),
        out_shape=(
            jax.ShapeDtypeStruct((all_rows, c), bf),
            jax.ShapeDtypeStruct((all_rows, d), bf),
            jax.ShapeDtypeStruct((principles * rk, d), f32),
            jax.ShapeDtypeStruct((principles * rk, c), f32),
        ),
        in_specs=[hbm] * 5 + [smem] * 2,
        out_specs=[hbm] * 4,
        scratch_shapes=[
            pltpu.VMEM((rows, d), bf),
            pltpu.VMEM((T, d, c), bf),
            pltpu.VMEM((T, rows, c), bf),
            pltpu.VMEM((principles, rank, d), bf),
            pltpu.VMEM((principles, rank, c), bf),
            pltpu.VMEM((nb, rank, d), bf),
            pltpu.VMEM((nb, rank, d), bf),
            pltpu.VMEM((nb, rank, d), bf),
            pltpu.VMEM((nb, rank, c), bf),
            pltpu.VMEM((nb, rank, c), bf),
            pltpu.VMEM((nb, rank, c), bf),
            pltpu.VMEM((rows, 2 * rank), bf),
            pltpu.VMEM((T, rows, 2 * rank), bf),
            pltpu.VMEM((rows, 2 * rank), bf),
            pltpu.VMEM((Z, nb * rk, d), bf),
            pltpu.VMEM((Z, nb * rk, c), bf),
            pltpu.VMEM((2 * nb * rk, 128), f32),
            pltpu.VMEM((Z, 2, nb * rk, d), bf),
            pltpu.VMEM((Z, 2, nb * rk, c), bf),
            pltpu.VMEM((Z, 2 * nb * rk, 128), f32),
            pltpu.VMEM((principles * rk, d), f32),
            pltpu.VMEM((principles * rk, c), f32),
            pltpu.VMEM((rows, d), f32),
            pltpu.VMEM((rows, c), f32),
            pltpu.VMEM((T, rows, c), bf),
            pltpu.VMEM((T, rows, c), bf),
            pltpu.VMEM((rows, c), bf),
            pltpu.VMEM((rows, d), bf),
            dma((12,)),
            dma((T,)),
            dma((T,)),
            dma((2,)),
            dma((2,)),
            dma((T,)),
            dma((T,)),
            dma((Z,)),
            dma((Z,)),
            dma((T,)),
            dma((T,)),
            dma((2,)),
            dma((2,)),
            dma((T,)),
            dma((T,)),
            dma((3, Z)),
            dma((3, Z)),
            dma((2, Z)),
            dma((2, Z)),
            dma((T,)),
            dma((T,)),
            dma((2,)),
            dma((2,)),
        ],
        compiler_params=pltpu.CompilerParams(
            collective_id=0, has_side_effects=True, vmem_limit_bytes=56 * 1024 * 1024
        ),
        cost_estimate=pl.CostEstimate(
            flops=4 * rows * d * c * T, bytes_accessed=8 * d * c * T, transcendentals=0
        ),
    )(
        tokens,
        frozen_weight,
        adapter_down_weight,
        adapter_up_weight,
        output_cotangent,
        principle_per_block,
        live_block_rows,
    )
    return out, hidden, dmap.reshape(principles, rk, d), umap.reshape(principles, rk, c)


def solution(mesh):
    in_specs = (
        P("dp", "tensor"),
        P(None, "tensor"),
        P("adapter", None, "tensor"),
        P("adapter", None, "tensor"),
        P("dp", "tensor"),
        P("dp"),
        P("dp"),
    )
    out_specs = (
        P("dp", "tensor"),
        P("dp", "tensor"),
        P("adapter", "dp", "tensor"),
        P("adapter", "dp", "tensor"),
    )
    return jax.shard_map(
        functools.partial(on_device, mesh.shape["tensor"], mesh.shape["dp"]),
        mesh=mesh,
        in_specs=in_specs,
        out_specs=out_specs,
        check_vma=False,
    )
```

```python
import functools

import jax
import jax.numpy as jnp
from jax import lax
from jax.experimental import pallas as pl
from jax.experimental.pallas import tpu as pltpu
from jax.sharding import PartitionSpec as P

BLOCK = 128
ADAPTER_SCALE = 2.0
MESH = pl.DeviceIdType.MESH


def flip(index, distance, count):
    out, bit = 0, 1
    while bit < count:
        out = out + ((index // bit + distance // bit) % 2) * bit
        bit *= 2
    return out


def tile_of(size, most):
    return most if size % most == 0 else size


def kernel(
    num_tensor,
    num_dp,
    tok_ref,
    w_ref,
    down_ref,
    up_ref,
    cot_ref,
    principle_ref,
    live_ref,
    out_ref,
    hid_ref,
    dmap_ref,
    umap_ref,
    tok_v,
    wf,
    cotf,
    down_v,
    up_v,
    a_snd,
    a_rcv,
    a_own,
    b_snd,
    b_rcv,
    b_own,
    rk_snd,
    rk_rcv,
    rank_v,
    gd_snd,
    gu_snd,
    ids_v,
    gdf,
    guf,
    gid,
    acc,
    o_zero,
    o_snd,
    o_rcv,
    loc_sem,
    cot_s,
    cot_r,
    cf_s,
    cf_r,
    w_s,
    w_r,
    wz_s,
    wz_r,
    wr_s,
    wr_r,
    ab_s,
    ab_r,
    rk_s,
    rk_r,
    g_s,
    g_r,
    gr_s,
    gr_r,
    o_s,
    o_r,
    fin_s,
    fin_r,
):
    z = lax.axis_index("dp")
    t = lax.axis_index("tensor")
    a = lax.axis_index("adapter")
    pa = 1 - a
    rows, d = tok_v.shape
    c = cotf.shape[2]
    half = d // 2
    nb = rows // BLOCK
    principles, rank = down_v.shape[:2]
    rk = rank // num_dp
    partner = (z, t, pa)
    my_rows = pl.ds(pl.multiple_of(a * rows, rows), rows)
    my_half = pl.ds(pl.multiple_of(a * half, half), half)

    def local(src, dst, sem):
        copy = pltpu.make_async_copy(src, dst, loc_sem.at[sem])
        copy.start()
        return copy

    def remote(src, dst, ss, rs, dev):
        copy = pltpu.make_async_remote_copy(
            src_ref=src, dst_ref=dst, send_sem=ss, recv_sem=rs, device_id=dev, device_id_type=MESH
        )
        copy.start()
        return copy

    cp_cot = local(cot_ref.at[my_rows, :], cotf.at[0], 0)
    cp_down = local(down_ref, down_v, 1)
    cp_up = local(up_ref, up_v, 2)
    cp_tok = local(tok_ref.at[my_rows, :], tok_v, 3)
    cp_w = local(w_ref.at[pl.ds(pl.multiple_of(t * d, d), d), :], wf.at[0], 4)

    tensor_peer = [None] + [(z, flip(t, k, num_tensor), a) for k in range(1, num_tensor)]
    dp_peer = [None] + [(lax.rem(z + j, num_dp), t, a) for j in range(1, num_dp)]
    barrier = pltpu.get_barrier_semaphore()
    for peer in tensor_peer[1:] + dp_peer[1:] + [partner]:
        pl.semaphore_signal(barrier, inc=1, device_id=peer, device_id_type=MESH)
    pl.semaphore_wait(barrier, num_tensor + num_dp - 1)

    far = num_tensor - 1
    share = half // num_dp
    my_share = pl.ds(pl.multiple_of(a * half + z * share, share), share)
    w_c = [None] * num_tensor
    far_at = pl.multiple_of(tensor_peer[far][1] * d + a * half + z * share, share)
    w_c[far] = remote(
        w_ref.at[pl.ds(far_at, share), :],
        wf.at[far, my_share, :],
        w_s.at[far],
        w_r.at[far],
        tensor_peer[far],
    )
    handed = num_tensor == 4
    cot_c = [None] * num_tensor
    for k in range(1, far if handed else num_tensor):
        cot_c[k] = remote(
            cot_ref.at[my_rows, :], cotf.at[k], cot_s.at[k], cot_r.at[k], tensor_peer[k]
        )

    def chosen(table, b):
        pick = principle_ref[b] - a * principles
        own = jnp.where((pick >= 0) & (pick < principles), 1.0, 0.0).astype(jnp.float32)
        pick = jnp.minimum(jnp.maximum(pick, 0), principles - 1)
        return (table[pick].astype(jnp.float32) * own).astype(jnp.bfloat16)

    cp_down.wait()
    cp_up.wait()
    for i in range(nb):
        a_snd[i] = chosen(down_v, pa * nb + i)
        b_snd[i] = chosen(up_v, pa * nb + i)
    a_c = remote(a_snd, a_rcv, ab_s.at[0], ab_r.at[0], partner)
    b_c = remote(b_snd, b_rcv, ab_s.at[1], ab_r.at[1], partner)
    for i in range(nb):
        a_own[i] = chosen(down_v, a * nb + i)
        b_own[i] = chosen(up_v, a * nb + i)
    for b in range(2 * nb):
        ids_v[b * rk : (b + 1) * rk, :] = jnp.full(
            (rk, 128), principle_ref[b].astype(jnp.float32), jnp.float32
        )
    w_c[far].wait_recv()
    wz_c = [None]
    for j in range(1, num_dp):
        mine = wf.at[far, my_share, :]
        wz_c.append(remote(mine, mine, wz_s.at[j], wz_r.at[j], dp_peer[j]))
    a_c.wait_recv()
    b_c.wait_recv()
    for i in range(nb):
        a_own[i] = a_own[i] + a_rcv[i]
        b_own[i] = b_own[i] + b_rcv[i]

    cp_tok.wait()
    cp_cot.wait()
    last = (((1,), (1,)), ((), ()))
    for i in range(nb):
        blk = slice(i * BLOCK, (i + 1) * BLOCK)
        low = lax.dot_general(tok_v[blk, :], a_own[i], last, preferred_element_type=jnp.float32)
        back = lax.dot_general(cotf[0, blk, :], b_own[i], last, preferred_element_type=jnp.float32)
        rk_snd[blk, :] = jnp.concatenate([low, back], axis=1).astype(jnp.bfloat16)
    rk_c = [None]
    for k in range(1, num_tensor):
        rk_c.append(remote(rk_snd, rk_rcv.at[k], rk_s.at[k], rk_r.at[k], tensor_peer[k]))
    for k in range(1, far):
        start = pl.multiple_of(tensor_peer[k][1] * d + a * half, half)
        w_c[k] = remote(
            w_ref.at[pl.ds(start, half), :],
            wf.at[k, my_half, :],
            w_s.at[k],
            w_r.at[k],
            tensor_peer[k],
        )
    cf_c = []
    if handed:
        for n, k in enumerate((1, 2)):
            cot_c[k].wait_recv()
            piece = slice(n * (rows // 2), (n + 1) * (rows // 2))
            cf_c.append(
                remote(
                    cotf.at[k, piece, :],
                    cotf.at[3, piece, :],
                    cf_s.at[n],
                    cf_r.at[n],
                    tensor_peer[3 - k],
                )
            )

    row_tile = tile_of(rows, 256)
    d_tile = tile_of(d, 512)

    def forward(k, store):
        @pl.loop(0, rows // row_tile)
        def _(step):
            at = pl.ds(pl.multiple_of(step * row_tile, row_tile), row_tile)
            store(at, jnp.dot(tok_v[at, :], wf[k], preferred_element_type=jnp.float32))

    def backward(k):
        @pl.loop(0, d // d_tile)
        def _(step):
            at = pl.ds(pl.multiple_of(step * d_tile, d_tile), d_tile)
            part = lax.dot_general(cotf[k], wf[k, at, :], last, preferred_element_type=jnp.float32)
            part = part.astype(jnp.bfloat16).astype(jnp.float32)
            acc[:, at] = part if k == 0 else acc[:, at] + part

    def store_zero(at, value):
        o_zero[at, :] = value

    cp_w.wait()
    forward(0, store_zero)
    backward(0)

    for k in range(1, num_tensor):
        rk_c[k].wait_recv()
    within = lax.broadcasted_iota(jnp.int32, (BLOCK, 2 * rank), 0)
    for i in range(nb):
        blk = slice(i * BLOCK, (i + 1) * BLOCK)
        total = rk_snd[blk, :].astype(jnp.float32)
        for k in range(1, num_tensor):
            total = total + rk_rcv[k, blk, :].astype(jnp.float32)
        total = jnp.where(within < live_ref[a * nb + i], total, 0.0)
        rank_v[blk, :] = total.astype(jnp.bfloat16)
        turned = total.T.astype(jnp.bfloat16)
        gd = jnp.dot(turned[rank:], tok_v[blk, :], preferred_element_type=jnp.float32)
        gu = jnp.dot(turned[:rank], cotf[0, blk, :], preferred_element_type=jnp.float32)
        gd = ADAPTER_SCALE * gd
        gu = ADAPTER_SCALE * gu
        for j in range(num_dp):
            part = slice(i * rk, (i + 1) * rk)
            gd_snd[j, part, :] = gd[j * rk : (j + 1) * rk].astype(jnp.bfloat16)
            gu_snd[j, part, :] = gu[j * rk : (j + 1) * rk].astype(jnp.bfloat16)
    g_c = [None]
    for j in range(1, num_dp):
        to = dp_peer[j][0]
        g_c.append(
            (
                remote(gd_snd.at[to], gdf.at[z, a], g_s.at[0, j], g_r.at[0, j], dp_peer[j]),
                remote(gu_snd.at[to], guf.at[z, a], g_s.at[1, j], g_r.at[1, j], dp_peer[j]),
                remote(ids_v, gid.at[z], g_s.at[2, j], g_r.at[2, j], dp_peer[j]),
            )
        )
    cp_gd = local(gd_snd.at[z], gdf.at[z, a], 1)
    cp_gu = local(gu_snd.at[z], guf.at[z, a], 2)
    cp_id = local(ids_v, gid.at[z], 0)
    gr_c = [
        (
            remote(gd_snd.at[z], gdf.at[z, a], gr_s.at[0, 0], gr_r.at[0, 0], partner),
            remote(gu_snd.at[z], guf.at[z, a], gr_s.at[1, 0], gr_r.at[1, 0], partner),
        )
    ]

    wr_c = [None] * num_tensor
    o_c = [None] * num_tensor

    def relay(k):
        if k == far:
            for j in range(1, num_dp):
                wz_c[j].wait_recv()
        else:
            w_c[k].wait_recv()
        wr_c[k] = remote(
            wf.at[k, my_half, :], wf.at[k, my_half, :], wr_s.at[k], wr_r.at[k], partner
        )

    relay(1)
    for k in range(1, num_tensor):
        if k + 1 < num_tensor and k < 2:
            relay(k + 1)
        wr_c[k].wait_recv()

        def store_send(at, value, k=k):
            o_snd[k, at, :] = value.astype(jnp.bfloat16)

        forward(k, store_send)
        o_c[k] = remote(o_snd.at[k], o_rcv.at[k], o_s.at[k], o_r.at[k], tensor_peer[k])
        if k >= 2 and k + 1 < num_tensor:
            relay(k + 1)
        if handed and k == far:
            for copy in cf_c:
                copy.wait_recv()
        elif not handed:
            cot_c[k].wait_recv()
        backward(k)

    for j in range(1, num_dp):
        for copy in g_c[j]:
            copy.wait_recv()
        source = lax.rem(z + num_dp - j, num_dp)
        mine_d, mine_u = gdf.at[source, a], guf.at[source, a]
        gr_c.append(
            (
                remote(mine_d, mine_d, gr_s.at[0, j], gr_r.at[0, j], partner),
                remote(mine_u, mine_u, gr_s.at[1, j], gr_r.at[1, j], partner),
            )
        )

    for i in range(nb):
        blk = slice(i * BLOCK, (i + 1) * BLOCK)
        low_b = rank_v[blk, :rank]
        back_b = rank_v[blk, rank:]
        term = jnp.dot(back_b, a_own[i], preferred_element_type=jnp.float32)
        at = pl.ds(pl.multiple_of(a * rows + i * BLOCK, BLOCK), BLOCK)
        hid_ref[at, :] = (acc[blk, :] + ADAPTER_SCALE * term).astype(jnp.bfloat16)
        o_term = jnp.dot(low_b, b_own[i], preferred_element_type=jnp.float32)
        o_zero[blk, :] = o_zero[blk, :] + ADAPTER_SCALE * o_term
    mine = hid_ref.at[my_rows, :]
    h_c = remote(mine, mine, fin_s.at[0], fin_r.at[0], partner)

    cp_gd.wait()
    cp_gu.wait()
    cp_id.wait()
    for pair in gr_c:
        for copy in pair:
            copy.wait_recv()
    held = num_dp * 2 * nb * rk
    width = principles * rk
    grads_d = gdf[...].reshape(held, d)
    grads_u = guf[...].reshape(held, c)
    ids = gid[...].reshape(held, 128)
    lane = lax.broadcasted_iota(jnp.int32, (held, 128), 1)
    sub = lax.broadcasted_iota(jnp.int32, (held, 128), 0)
    for part in range(width // 128):
        to = slice(part * 128 // rk, (part + 1) * 128 // rk)
        column = lane + part * 128
        slot = (a * principles + column // rk).astype(jnp.float32)
        hit = (ids == slot) & (column % rk == sub % rk)
        select = jnp.where(hit, 1.0, 0.0).astype(jnp.float32).T.astype(jnp.bfloat16)
        down = jnp.dot(select, grads_d, preferred_element_type=jnp.float32)
        dmap_ref[to] = down.reshape(128 // rk, rk, d)
        up = jnp.dot(select, grads_u, preferred_element_type=jnp.float32)
        umap_ref[to] = up.reshape(128 // rk, rk, c)

    for k in range(1, num_tensor):
        o_c[k].wait_recv()
    for i in range(nb):
        blk = slice(i * BLOCK, (i + 1) * BLOCK)
        total = o_zero[blk, :]
        for k in range(1, num_tensor):
            total = total + o_rcv[k, blk, :].astype(jnp.float32)
        at = pl.ds(pl.multiple_of(a * rows + i * BLOCK, BLOCK), BLOCK)
        out_ref[at, :] = total.astype(jnp.bfloat16)
    mine = out_ref.at[my_rows, :]
    of_c = remote(mine, mine, fin_s.at[1], fin_r.at[1], partner)

    for k in range(1, num_tensor):
        if cot_c[k] is not None:
            cot_c[k].wait_send()
        w_c[k].wait_send()
        rk_c[k].wait_send()
        wr_c[k].wait_send()
        o_c[k].wait_send()
    for copy in cf_c:
        copy.wait_send()
    a_c.wait_send()
    b_c.wait_send()
    for j in range(1, num_dp):
        for copy in g_c[j]:
            copy.wait_send()
        wz_c[j].wait_send()
    for pair in gr_c:
        for copy in pair:
            copy.wait_send()
    h_c.wait()
    of_c.wait()


def write_out(*refs):
    copies = [pltpu.make_async_copy(refs[n], refs[4 + n], refs[8].at[n]) for n in range(4)]
    for copy in copies:
        copy.start()
    for copy in copies:
        copy.wait()


def on_device(
    num_tensor,
    num_dp,
    tokens,
    frozen_weight,
    adapter_down_weight,
    adapter_up_weight,
    output_cotangent,
    principle_per_block,
    live_block_rows,
):
    all_rows, d = tokens.shape
    c = frozen_weight.shape[1]
    principles, rank = adapter_down_weight.shape[:2]
    blocks = all_rows // BLOCK
    rows, nb, rk = all_rows // 2, blocks // 2, rank // num_dp
    bf, f32 = jnp.bfloat16, jnp.float32
    hbm = pl.BlockSpec(memory_space=pl.ANY)
    vmem = pl.BlockSpec(memory_space=pltpu.VMEM)
    smem = pl.BlockSpec(memory_space=pltpu.SMEM)
    dma = pltpu.SemaphoreType.DMA
    T, Z = num_tensor, num_dp
    results = pl.pallas_call(
        functools.partial(kernel, T, Z),
        out_shape=(
            pltpu.VMEM((all_rows, c), bf),
            pltpu.VMEM((all_rows, d), bf),
            pltpu.VMEM((principles, rk, d), f32),
            pltpu.VMEM((principles, rk, c), f32),
        ),
        in_specs=[hbm] * 5 + [smem] * 2,
        out_specs=[vmem] * 4,
        scratch_shapes=[
            pltpu.VMEM((rows, d), bf),
            pltpu.VMEM((T, d, c), bf),
            pltpu.VMEM((T, rows, c), bf),
            pltpu.VMEM((principles, rank, d), bf),
            pltpu.VMEM((principles, rank, c), bf),
            pltpu.VMEM((nb, rank, d), bf),
            pltpu.VMEM((nb, rank, d), bf),
            pltpu.VMEM((nb, rank, d), bf),
            pltpu.VMEM((nb, rank, c), bf),
            pltpu.VMEM((nb, rank, c), bf),
            pltpu.VMEM((nb, rank, c), bf),
            pltpu.VMEM((rows, 2 * rank), bf),
            pltpu.VMEM((T, rows, 2 * rank), bf),
            pltpu.VMEM((rows, 2 * rank), bf),
            pltpu.VMEM((Z, nb * rk, d), bf),
            pltpu.VMEM((Z, nb * rk, c), bf),
            pltpu.VMEM((2 * nb * rk, 128), f32),
            pltpu.VMEM((Z, 2, nb * rk, d), bf),
            pltpu.VMEM((Z, 2, nb * rk, c), bf),
            pltpu.VMEM((Z, 2 * nb * rk, 128), f32),
            pltpu.VMEM((rows, d), f32),
            pltpu.VMEM((rows, c), f32),
            pltpu.VMEM((T, rows, c), bf),
            pltpu.VMEM((T, rows, c), bf),
            dma((5,)),
            dma((T,)),
            dma((T,)),
            dma((2,)),
            dma((2,)),
            dma((T,)),
            dma((T,)),
            dma((Z,)),
            dma((Z,)),
            dma((T,)),
            dma((T,)),
            dma((2,)),
            dma((2,)),
            dma((T,)),
            dma((T,)),
            dma((3, Z)),
            dma((3, Z)),
            dma((2, Z)),
            dma((2, Z)),
            dma((T,)),
            dma((T,)),
            dma((2,)),
            dma((2,)),
        ],
        compiler_params=pltpu.CompilerParams(
            collective_id=0, has_side_effects=True, vmem_limit_bytes=46 * 1024 * 1024
        ),
        cost_estimate=pl.CostEstimate(
            flops=4 * rows * d * c * T, bytes_accessed=8 * d * c * T, transcendentals=0
        ),
    )(
        tokens,
        frozen_weight,
        adapter_down_weight,
        adapter_up_weight,
        output_cotangent,
        principle_per_block,
        live_block_rows,
    )
    return pl.pallas_call(
        write_out,
        out_shape=tuple(jax.ShapeDtypeStruct(r.shape, r.dtype) for r in results),
        in_specs=[vmem] * 4,
        out_specs=[hbm] * 4,
        scratch_shapes=[dma((4,))],
    )(*results)


def solution(mesh):
    in_specs = (
        P("dp", "tensor"),
        P(None, "tensor"),
        P("adapter", None, "tensor"),
        P("adapter", None, "tensor"),
        P("dp", "tensor"),
        P("dp"),
        P("dp"),
    )
    out_specs = (
        P("dp", "tensor"),
        P("dp", "tensor"),
        P("adapter", "dp", "tensor"),
        P("adapter", "dp", "tensor"),
    )
    return jax.shard_map(
        functools.partial(on_device, mesh.shape["tensor"], mesh.shape["dp"]),
        mesh=mesh,
        in_specs=in_specs,
        out_specs=out_specs,
        check_vma=False,
    )
```

```python
import functools

import jax
import jax.numpy as jnp
from jax import lax
from jax.experimental import pallas as pl
from jax.experimental.pallas import tpu as pltpu
from jax.sharding import PartitionSpec as P

BLOCK = 128
ADAPTER_SCALE = 2.0
MESH = pl.DeviceIdType.MESH


def flip(index, distance, count):
    out, bit = 0, 1
    while bit < count:
        out = out + ((index // bit + distance // bit) % 2) * bit
        bit *= 2
    return out


def tile_of(size, most):
    return most if size % most == 0 else size


def kernel(
    num_tensor,
    num_dp,
    tok_ref,
    w_ref,
    down_ref,
    up_ref,
    cot_ref,
    principle_ref,
    live_ref,
    out_ref,
    hid_ref,
    dmap_ref,
    umap_ref,
    tok_v,
    wf,
    cotf,
    down_v,
    up_v,
    a_snd,
    a_rcv,
    a_own,
    b_snd,
    b_rcv,
    b_own,
    rk_snd,
    rk_rcv,
    rank_v,
    gd_snd,
    gu_snd,
    ids_v,
    gdf,
    guf,
    gid,
    acc,
    o_zero,
    o_snd,
    o_rcv,
    loc_sem,
    cot_s,
    cot_r,
    cf_s,
    cf_r,
    w_s,
    w_r,
    wz_s,
    wz_r,
    wr_s,
    wr_r,
    ab_s,
    ab_r,
    rk_s,
    rk_r,
    g_s,
    g_r,
    gr_s,
    gr_r,
    o_s,
    o_r,
    fin_s,
    fin_r,
):
    z = lax.axis_index("dp")
    t = lax.axis_index("tensor")
    a = lax.axis_index("adapter")
    pa = 1 - a
    rows, d = tok_v.shape
    c = cotf.shape[2]
    half = d // 2
    nb = rows // BLOCK
    principles, rank = down_v.shape[:2]
    rk = rank // num_dp
    partner = (z, t, pa)
    my_rows = pl.ds(pl.multiple_of(a * rows, rows), rows)
    my_half = pl.ds(pl.multiple_of(a * half, half), half)

    def local(src, dst, sem):
        copy = pltpu.make_async_copy(src, dst, loc_sem.at[sem])
        copy.start()
        return copy

    def remote(src, dst, ss, rs, dev):
        copy = pltpu.make_async_remote_copy(
            src_ref=src, dst_ref=dst, send_sem=ss, recv_sem=rs, device_id=dev, device_id_type=MESH
        )
        copy.start()
        return copy

    cp_cot = local(cot_ref.at[my_rows, :], cotf.at[0], 0)
    cp_down = local(down_ref, down_v, 1)
    cp_up = local(up_ref, up_v, 2)
    cp_tok = local(tok_ref.at[my_rows, :], tok_v, 3)
    cp_w = local(w_ref.at[pl.ds(pl.multiple_of(t * d, d), d), :], wf.at[0], 4)

    tensor_peer = [None] + [(z, flip(t, k, num_tensor), a) for k in range(1, num_tensor)]
    dp_peer = [None] + [(lax.rem(z + j, num_dp), t, a) for j in range(1, num_dp)]
    barrier = pltpu.get_barrier_semaphore()
    for peer in tensor_peer[1:] + dp_peer[1:] + [partner]:
        pl.semaphore_signal(barrier, inc=1, device_id=peer, device_id_type=MESH)
    pl.semaphore_wait(barrier, num_tensor + num_dp - 1)

    far = num_tensor - 1
    share = half // num_dp
    my_share = pl.ds(pl.multiple_of(a * half + z * share, share), share)
    w_c = [None] * num_tensor
    far_at = pl.multiple_of(tensor_peer[far][1] * d + a * half + z * share, share)
    w_c[far] = remote(
        w_ref.at[pl.ds(far_at, share), :],
        wf.at[far, my_share, :],
        w_s.at[far],
        w_r.at[far],
        tensor_peer[far],
    )
    handed = num_tensor == 4
    cot_c = [None] * num_tensor
    for k in range(1, far if handed else num_tensor):
        cot_c[k] = remote(
            cot_ref.at[my_rows, :], cotf.at[k], cot_s.at[k], cot_r.at[k], tensor_peer[k]
        )

    def chosen(table, b):
        pick = principle_ref[b] - a * principles
        own = jnp.where((pick >= 0) & (pick < principles), 1.0, 0.0).astype(jnp.float32)
        pick = jnp.minimum(jnp.maximum(pick, 0), principles - 1)
        return (table[pick].astype(jnp.float32) * own).astype(jnp.bfloat16)

    cp_down.wait()
    cp_up.wait()
    for i in range(nb):
        a_snd[i] = chosen(down_v, pa * nb + i)
        b_snd[i] = chosen(up_v, pa * nb + i)
    a_c = remote(a_snd, a_rcv, ab_s.at[0], ab_r.at[0], partner)
    b_c = remote(b_snd, b_rcv, ab_s.at[1], ab_r.at[1], partner)
    for i in range(nb):
        a_own[i] = chosen(down_v, a * nb + i)
        b_own[i] = chosen(up_v, a * nb + i)
    for b in range(2 * nb):
        ids_v[b * rk : (b + 1) * rk, :] = jnp.full(
            (rk, 128), principle_ref[b].astype(jnp.float32), jnp.float32
        )
    w_c[far].wait_recv()
    wz_c = [None]
    for j in range(1, num_dp):
        mine = wf.at[far, my_share, :]
        wz_c.append(remote(mine, mine, wz_s.at[j], wz_r.at[j], dp_peer[j]))
    a_c.wait_recv()
    b_c.wait_recv()
    for i in range(nb):
        a_own[i] = a_own[i] + a_rcv[i]
        b_own[i] = b_own[i] + b_rcv[i]

    cp_tok.wait()
    cp_cot.wait()
    last = (((1,), (1,)), ((), ()))
    for i in range(nb):
        blk = slice(i * BLOCK, (i + 1) * BLOCK)
        low = lax.dot_general(tok_v[blk, :], a_own[i], last, preferred_element_type=jnp.float32)
        back = lax.dot_general(cotf[0, blk, :], b_own[i], last, preferred_element_type=jnp.float32)
        rk_snd[blk, :] = jnp.concatenate([low, back], axis=1).astype(jnp.bfloat16)
    rk_c = [None]
    for k in range(1, num_tensor):
        rk_c.append(remote(rk_snd, rk_rcv.at[k], rk_s.at[k], rk_r.at[k], tensor_peer[k]))
    for k in range(1, far):
        start = pl.multiple_of(tensor_peer[k][1] * d + a * half, half)
        w_c[k] = remote(
            w_ref.at[pl.ds(start, half), :],
            wf.at[k, my_half, :],
            w_s.at[k],
            w_r.at[k],
            tensor_peer[k],
        )
    cf_c = []
    if handed:
        for n, k in enumerate((1, 2)):
            cot_c[k].wait_recv()
            piece = slice(n * (rows // 2), (n + 1) * (rows // 2))
            cf_c.append(
                remote(
                    cotf.at[k, piece, :],
                    cotf.at[3, piece, :],
                    cf_s.at[n],
                    cf_r.at[n],
                    tensor_peer[3 - k],
                )
            )

    row_tile = tile_of(rows, 256)
    d_tile = tile_of(d, 512)

    def forward(k, store):
        @pl.loop(0, rows // row_tile)
        def _(step):
            at = pl.ds(pl.multiple_of(step * row_tile, row_tile), row_tile)
            store(at, jnp.dot(tok_v[at, :], wf[k], preferred_element_type=jnp.float32))

    def backward(k):
        @pl.loop(0, d // d_tile)
        def _(step):
            at = pl.ds(pl.multiple_of(step * d_tile, d_tile), d_tile)
            part = lax.dot_general(cotf[k], wf[k, at, :], last, preferred_element_type=jnp.float32)
            part = part.astype(jnp.bfloat16).astype(jnp.float32)
            acc[:, at] = part if k == 0 else acc[:, at] + part

    def store_zero(at, value):
        o_zero[at, :] = value

    cp_w.wait()
    forward(0, store_zero)
    backward(0)

    for k in range(1, num_tensor):
        rk_c[k].wait_recv()
    within = lax.broadcasted_iota(jnp.int32, (BLOCK, 2 * rank), 0)
    for i in range(nb):
        blk = slice(i * BLOCK, (i + 1) * BLOCK)
        total = rk_snd[blk, :].astype(jnp.float32)
        for k in range(1, num_tensor):
            total = total + rk_rcv[k, blk, :].astype(jnp.float32)
        total = jnp.where(within < live_ref[a * nb + i], total, 0.0)
        rank_v[blk, :] = total.astype(jnp.bfloat16)
        turned = total.T.astype(jnp.bfloat16)
        gd = jnp.dot(turned[rank:], tok_v[blk, :], preferred_element_type=jnp.float32)
        gu = jnp.dot(turned[:rank], cotf[0, blk, :], preferred_element_type=jnp.float32)
        gd = ADAPTER_SCALE * gd
        gu = ADAPTER_SCALE * gu
        for j in range(num_dp):
            part = slice(i * rk, (i + 1) * rk)
            gd_snd[j, part, :] = gd[j * rk : (j + 1) * rk].astype(jnp.bfloat16)
            gu_snd[j, part, :] = gu[j * rk : (j + 1) * rk].astype(jnp.bfloat16)
    g_c = [None]
    for j in range(1, num_dp):
        to = dp_peer[j][0]
        g_c.append(
            (
                remote(gd_snd.at[to], gdf.at[z, a], g_s.at[0, j], g_r.at[0, j], dp_peer[j]),
                remote(gu_snd.at[to], guf.at[z, a], g_s.at[1, j], g_r.at[1, j], dp_peer[j]),
                remote(ids_v, gid.at[z], g_s.at[2, j], g_r.at[2, j], dp_peer[j]),
            )
        )
    cp_gd = local(gd_snd.at[z], gdf.at[z, a], 1)
    cp_gu = local(gu_snd.at[z], guf.at[z, a], 2)
    cp_id = local(ids_v, gid.at[z], 0)
    gr_c = [
        (
            remote(gd_snd.at[z], gdf.at[z, a], gr_s.at[0, 0], gr_r.at[0, 0], partner),
            remote(gu_snd.at[z], guf.at[z, a], gr_s.at[1, 0], gr_r.at[1, 0], partner),
        )
    ]

    wr_c = [None] * num_tensor
    o_c = [None] * num_tensor

    def relay(k):
        if k == far:
            for j in range(1, num_dp):
                wz_c[j].wait_recv()
        else:
            w_c[k].wait_recv()
        wr_c[k] = remote(
            wf.at[k, my_half, :], wf.at[k, my_half, :], wr_s.at[k], wr_r.at[k], partner
        )

    relay(1)
    for k in range(1, num_tensor):
        if k + 1 < num_tensor and k < 2:
            relay(k + 1)
        wr_c[k].wait_recv()

        def store_send(at, value, k=k):
            o_snd[k, at, :] = value.astype(jnp.bfloat16)

        forward(k, store_send)
        o_c[k] = remote(o_snd.at[k], o_rcv.at[k], o_s.at[k], o_r.at[k], tensor_peer[k])
        if k >= 2 and k + 1 < num_tensor:
            relay(k + 1)
        if handed and k == far:
            for copy in cf_c:
                copy.wait_recv()
        elif not handed:
            cot_c[k].wait_recv()
        backward(k)

    for j in range(1, num_dp):
        for copy in g_c[j]:
            copy.wait_recv()
        source = lax.rem(z + num_dp - j, num_dp)
        mine_d, mine_u = gdf.at[source, a], guf.at[source, a]
        gr_c.append(
            (
                remote(mine_d, mine_d, gr_s.at[0, j], gr_r.at[0, j], partner),
                remote(mine_u, mine_u, gr_s.at[1, j], gr_r.at[1, j], partner),
            )
        )

    for i in range(nb):
        blk = slice(i * BLOCK, (i + 1) * BLOCK)
        low_b = rank_v[blk, :rank]
        back_b = rank_v[blk, rank:]
        term = jnp.dot(back_b, a_own[i], preferred_element_type=jnp.float32)
        at = pl.ds(pl.multiple_of(a * rows + i * BLOCK, BLOCK), BLOCK)
        hid_ref[at, :] = (acc[blk, :] + ADAPTER_SCALE * term).astype(jnp.bfloat16)
        o_term = jnp.dot(low_b, b_own[i], preferred_element_type=jnp.float32)
        o_zero[blk, :] = o_zero[blk, :] + ADAPTER_SCALE * o_term
    mine = hid_ref.at[my_rows, :]
    h_c = remote(mine, mine, fin_s.at[0], fin_r.at[0], partner)

    cp_gd.wait()
    cp_gu.wait()
    cp_id.wait()
    for pair in gr_c:
        for copy in pair:
            copy.wait_recv()
    held = num_dp * 2 * nb * rk
    width = principles * rk
    grads_d = gdf[...].reshape(held, d)
    grads_u = guf[...].reshape(held, c)
    ids = gid[...].reshape(held, 128)
    lane = lax.broadcasted_iota(jnp.int32, (held, 128), 1)
    sub = lax.broadcasted_iota(jnp.int32, (held, 128), 0)
    for part in range(width // 128):
        to = slice(part * 128 // rk, (part + 1) * 128 // rk)
        column = lane + part * 128
        slot = (a * principles + column // rk).astype(jnp.float32)
        hit = (ids == slot) & (column % rk == sub % rk)
        select = jnp.where(hit, 1.0, 0.0).astype(jnp.float32).T.astype(jnp.bfloat16)
        down = jnp.dot(select, grads_d, preferred_element_type=jnp.float32)
        dmap_ref[to] = down.reshape(128 // rk, rk, d)
        up = jnp.dot(select, grads_u, preferred_element_type=jnp.float32)
        umap_ref[to] = up.reshape(128 // rk, rk, c)

    for k in range(1, num_tensor):
        o_c[k].wait_recv()
    for i in range(nb):
        blk = slice(i * BLOCK, (i + 1) * BLOCK)
        total = o_zero[blk, :]
        for k in range(1, num_tensor):
            total = total + o_rcv[k, blk, :].astype(jnp.float32)
        at = pl.ds(pl.multiple_of(a * rows + i * BLOCK, BLOCK), BLOCK)
        out_ref[at, :] = total.astype(jnp.bfloat16)
    mine = out_ref.at[my_rows, :]
    of_c = remote(mine, mine, fin_s.at[1], fin_r.at[1], partner)

    for k in range(1, num_tensor):
        if cot_c[k] is not None:
            cot_c[k].wait_send()
        w_c[k].wait_send()
        rk_c[k].wait_send()
        wr_c[k].wait_send()
        o_c[k].wait_send()
    for copy in cf_c:
        copy.wait_send()
    a_c.wait_send()
    b_c.wait_send()
    for j in range(1, num_dp):
        for copy in g_c[j]:
            copy.wait_send()
        wz_c[j].wait_send()
    for pair in gr_c:
        for copy in pair:
            copy.wait_send()
    h_c.wait()
    of_c.wait()


def write_out(*refs):
    copies = [pltpu.make_async_copy(refs[n], refs[4 + n], refs[8].at[n]) for n in range(4)]
    for copy in copies:
        copy.start()
    for copy in copies:
        copy.wait()


def on_device(
    num_tensor,
    num_dp,
    tokens,
    frozen_weight,
    adapter_down_weight,
    adapter_up_weight,
    output_cotangent,
    principle_per_block,
    live_block_rows,
):
    all_rows, d = tokens.shape
    c = frozen_weight.shape[1]
    principles, rank = adapter_down_weight.shape[:2]
    blocks = all_rows // BLOCK
    rows, nb, rk = all_rows // 2, blocks // 2, rank // num_dp
    bf, f32 = jnp.bfloat16, jnp.float32
    hbm = pl.BlockSpec(memory_space=pl.ANY)
    vmem = pl.BlockSpec(memory_space=pltpu.VMEM)
    smem = pl.BlockSpec(memory_space=pltpu.SMEM)
    dma = pltpu.SemaphoreType.DMA
    T, Z = num_tensor, num_dp
    results = pl.pallas_call(
        functools.partial(kernel, T, Z),
        out_shape=(
            pltpu.VMEM((all_rows, c), bf),
            pltpu.VMEM((all_rows, d), bf),
            pltpu.VMEM((principles, rk, d), f32),
            pltpu.VMEM((principles, rk, c), f32),
        ),
        in_specs=[hbm] * 5 + [smem] * 2,
        out_specs=[vmem] * 4,
        scratch_shapes=[
            pltpu.VMEM((rows, d), bf),
            pltpu.VMEM((T, d, c), bf),
            pltpu.VMEM((T, rows, c), bf),
            pltpu.VMEM((principles, rank, d), bf),
            pltpu.VMEM((principles, rank, c), bf),
            pltpu.VMEM((nb, rank, d), bf),
            pltpu.VMEM((nb, rank, d), bf),
            pltpu.VMEM((nb, rank, d), bf),
            pltpu.VMEM((nb, rank, c), bf),
            pltpu.VMEM((nb, rank, c), bf),
            pltpu.VMEM((nb, rank, c), bf),
            pltpu.VMEM((rows, 2 * rank), bf),
            pltpu.VMEM((T, rows, 2 * rank), bf),
            pltpu.VMEM((rows, 2 * rank), bf),
            pltpu.VMEM((Z, nb * rk, d), bf),
            pltpu.VMEM((Z, nb * rk, c), bf),
            pltpu.VMEM((2 * nb * rk, 128), f32),
            pltpu.VMEM((Z, 2, nb * rk, d), bf),
            pltpu.VMEM((Z, 2, nb * rk, c), bf),
            pltpu.VMEM((Z, 2 * nb * rk, 128), f32),
            pltpu.VMEM((rows, d), f32),
            pltpu.VMEM((rows, c), f32),
            pltpu.VMEM((T, rows, c), bf),
            pltpu.VMEM((T, rows, c), bf),
            dma((5,)),
            dma((T,)),
            dma((T,)),
            dma((2,)),
            dma((2,)),
            dma((T,)),
            dma((T,)),
            dma((Z,)),
            dma((Z,)),
            dma((T,)),
            dma((T,)),
            dma((2,)),
            dma((2,)),
            dma((T,)),
            dma((T,)),
            dma((3, Z)),
            dma((3, Z)),
            dma((2, Z)),
            dma((2, Z)),
            dma((T,)),
            dma((T,)),
            dma((2,)),
            dma((2,)),
        ],
        compiler_params=pltpu.CompilerParams(
            collective_id=0, has_side_effects=True, vmem_limit_bytes=46 * 1024 * 1024
        ),
        cost_estimate=pl.CostEstimate(
            flops=4 * rows * d * c * T, bytes_accessed=8 * d * c * T, transcendentals=0
        ),
    )(
        tokens,
        frozen_weight,
        adapter_down_weight,
        adapter_up_weight,
        output_cotangent,
        principle_per_block,
        live_block_rows,
    )
    return pl.pallas_call(
        write_out,
        out_shape=tuple(jax.ShapeDtypeStruct(r.shape, r.dtype) for r in results),
        in_specs=[vmem] * 4,
        out_specs=[hbm] * 4,
        scratch_shapes=[dma((4,))],
        compiler_params=pltpu.CompilerParams(vmem_limit_bytes=1024 * 1024),
    )(*results)


def solution(mesh):
    in_specs = (
        P("dp", "tensor"),
        P(None, "tensor"),
        P("adapter", None, "tensor"),
        P("adapter", None, "tensor"),
        P("dp", "tensor"),
        P("dp"),
        P("dp"),
    )
    out_specs = (
        P("dp", "tensor"),
        P("dp", "tensor"),
        P("adapter", "dp", "tensor"),
        P("adapter", "dp", "tensor"),
    )
    return jax.shard_map(
        functools.partial(on_device, mesh.shape["tensor"], mesh.shape["dp"]),
        mesh=mesh,
        in_specs=in_specs,
        out_specs=out_specs,
        check_vma=False,
    )
```
